32 devices in a mesh: row: 4 (over y, core), col: 8 (over z, x).
Axes of the slice: x: 2, y: 2, z: 4, core: 2. Of those that a mesh axis runs over, the one named last changes fastest.
Arguments:
- query_grads: bfloat16 [256, 8192], P('row', 'col'), may hold values from -6 to 6
- query_acts: bfloat16 [256, 8192], P('col', 'row'), may hold values from -6 to 6
- train_grads: bfloat16 [512, 8192], P('row', 'col'), may hold values from -6 to 6
- train_acts: bfloat16 [512, 8192], P('col', 'row'), may hold values from -6 to 6
- grad_basis: bfloat16 [8192, 8192], P('col', 'row'), may hold values from -0.0625 to 0.0625
- act_basis: bfloat16 [8192, 8192], P('row', 'col'), may hold values from -0.0625 to 0.0625
- eigen_corr: float32 [8192, 8192], P('row', 'col'), may hold values from 0.02 to 2
- damping: float32 [], replicated, may hold values from 0.05 to 0.5
- query_seq: int32 [256], replicated, may hold values from 0 to 31, never falling along the last dimension, each value on 1 to 16 neighbouring positions
- train_doc: int32 [512], replicated, may hold values from 0 to 15, never falling along the last dimension, each value on 1 to 64 neighbouring positions
Outputs:
- scores: float32 [32, 512], P(None, 'col')
- doc_scores: float32 [32, 16], replicated
The draws below stay inside these ranges and needn't reach their ends.
Inputs may be any that keep to these rules, and one draw needn't show every extreme that they name: `query_seq`: Non-decreasing along the query tokens; every sequence has 1 to 16 tokens, and one has exactly that many. `train_doc`: Non-decreasing along the training tokens; every document has 1 to 64 tokens, and one has exactly that many.
All inputs are finite; a program needn't handle non-finite values.
Results may differ from the reference program's by a relative error of at most 0.005.
Values may be sent and summed in bfloat16 or wider, within the bound.
A program may use at most 64 MiB of HBM per device.

```python
import math
import jax
import jax.numpy as jnp
import numpy as np
from jax import lax

D = 8192
S = 32
QTOK = 256
UTOK = 512
DOCS = 16


def block_scale(rng, dims, split, least, largest):
    factor_of, own = 1.0, jax.random.fold_in(rng, 6)
    for position, shards_of in split:
        steps = jnp.exp(jax.random.uniform(jax.random.fold_in(own, position), (shards_of,), jnp.float32, least / len(split), largest / len(split)))
        factor_of = factor_of * jnp.repeat(steps, dims[position] // shards_of).reshape([-1 if axis == position else 1 for axis in range(len(dims))])
    return factor_of


def length_profile(count, total, most, lean):
    loads = [(1 << 20) // math.isqrt(standing ** lean) + 1 for standing in range(2, count + 1)]
    spare, holding = total - most - (count - 1), [1] * (count - 1)
    while spare > 0:
        candidates = [i for i in range(count - 1) if holding[i] < most]
        mass, remaining = sum([loads[i] for i in candidates]), spare
        for i in candidates:
            addition = min(most - holding[i], max(1, remaining * loads[i] // mass), spare)
            holding[i] = holding[i] + addition
            spare = spare - addition
    return np.array([most] + holding)


def uneven(stream_key, count, total, limit, skew):
    if count == 2:
        one = jax.random.randint(stream_key, (), max(1, total - limit), min(limit, total - 1) + 1)
        return jnp.stack([one, total - one])
    lengths = jnp.asarray(length_profile(count, total, limit, skew), jnp.int32)
    pairs = (count - 1) // 2
    donor, taker = lengths[1:1 + 2 * pairs:2], lengths[2:2 + 2 * pairs:2]
    margin = jnp.minimum(donor - 1, limit - taker)
    shifted = jax.random.randint(jax.random.fold_in(stream_key, 1), (pairs,), 0, 1 << 20) % (margin + 1)
    lengths = lengths.at[1:1 + 2 * pairs:2].set(donor - shifted).at[2:2 + 2 * pairs:2].set(taker + shifted)
    return lengths[jax.random.permutation(jax.random.fold_in(stream_key, 2), count)]


def normal_values(key, shape, width, bound, split=(), held_as=jnp.bfloat16):
    array = jax.random.normal(key, shape, jnp.float32) * width
    if len(split) > 0:
        array = block_scale(key, shape, split, -0.22, 0.18) * array
    return jnp.clip(array, min=-bound, max=bound).astype(held_as)


def setup_inputs(seed: int = 0) -> dict:
    arg_keys = jax.random.split(jax.random.key(seed), 11)
    query_grads = normal_values(arg_keys[0], (QTOK, D), 1.0, 6.0, ((0, 4), (1, 8)))
    query_acts = normal_values(arg_keys[1], (QTOK, D), 1.0, 6.0, ((0, 8), (1, 4)))
    train_grads = normal_values(arg_keys[2], (UTOK, D), 1.0, 6.0, ((0, 4), (1, 8)))
    train_acts = normal_values(arg_keys[3], (UTOK, D), 1.0, 6.0, ((0, 8), (1, 4)))
    grad_basis = normal_values(arg_keys[4], (D, D), D ** -0.5, 0.0625, ((0, 8), (1, 4)))
    act_basis = normal_values(arg_keys[5], (D, D), D ** -0.5, 0.0625, ((0, 4), (1, 8)))
    eigen_corr = jnp.clip(jnp.exp(math.log(2.0) - 4.6051702 * jax.random.uniform(arg_keys[6], (D, D), jnp.float32) ** block_scale(arg_keys[6], (D, D), ((0, 4), (1, 8)), -0.2, 0.2)), 0.02, 2.0)
    damping = jnp.clip(jax.random.uniform(arg_keys[7], (), jnp.float32, 0.05, 0.5), 0.05, 0.5)
    query_seq = jnp.searchsorted(jnp.cumsum(uneven(arg_keys[8], S, QTOK, 2 * QTOK // S, 1)), jnp.arange(QTOK), side="right").astype(jnp.int32)
    train_doc = jnp.searchsorted(jnp.cumsum(uneven(arg_keys[9], DOCS, UTOK, 2 * UTOK // DOCS, 1)), jnp.arange(UTOK), side="right").astype(jnp.int32)
    return {"query_grads": query_grads, "query_acts": query_acts, "train_grads": train_grads, "train_acts": train_acts, "grad_basis": grad_basis, "act_basis": act_basis, "eigen_corr": eigen_corr, "damping": damping, "query_seq": query_seq, "train_doc": train_doc}


def reference(query_grads, query_acts, train_grads, train_acts, grad_basis, act_basis, eigen_corr, damping, query_seq, train_doc):
    grad_query = jnp.dot(query_grads, grad_basis, preferred_element_type=jnp.float32).astype(jnp.bfloat16)
    grad_train = jnp.dot(train_grads, grad_basis, preferred_element_type=jnp.float32).astype(jnp.bfloat16)
    act_query = jnp.dot(query_acts, act_basis, preferred_element_type=jnp.float32).astype(jnp.bfloat16)
    act_train = jnp.dot(train_acts, act_basis, preferred_element_type=jnp.float32).astype(jnp.bfloat16)
    denom = eigen_corr + damping
    act_wide = act_train.astype(jnp.float32)

    def one_sequence(seq_index):
        member = (query_seq == seq_index).astype(jnp.bfloat16)
        weighted = grad_query * member[:, None]
        outer = jnp.dot(weighted.T, act_query, preferred_element_type=jnp.float32)
        precond = (outer / denom).astype(jnp.bfloat16)
        mapped = jnp.dot(grad_train, precond, preferred_element_type=jnp.float32)
        return jnp.sum(mapped * act_wide, axis=1) / D

    scores = lax.map(one_sequence, jnp.arange(S, dtype=jnp.int32))
    doc_table = (train_doc[:, None] == jnp.arange(DOCS, dtype=jnp.int32)[None, :]).astype(jnp.float32)
    counts = jnp.sum(doc_table, axis=0)
    doc_sum = jnp.dot(scores, doc_table, precision=lax.Precision.HIGHEST)
    return scores, doc_sum / counts[None, :]
```

```python
import functools

import jax
import jax.numpy as jnp
from jax import lax
from jax.experimental import pallas as pl
from jax.experimental.pallas import tpu as pltpu
from jax.sharding import PartitionSpec as P

D = 8192
S = 32
DOCS = 16
CHUNKS = 4


def score_kernel(n_seq, n_query, sub, damp_ref, seq_ref, grad_ref, aq_ref, au_ref, eig_ref, out_ref,
                 inv_ref, wide_ref, even_ref, odd_ref):
    rows, cols = eig_ref.shape
    n_train = au_ref.shape[1]
    inv_ref[...] = 1.0 / (eig_ref[...] + damp_ref[0, 0])
    wide_ref[...] = grad_ref[:, n_query:].astype(jnp.float32)

    def precondition(s, p_ref):
        member = (seq_ref[...] == s).astype(jnp.float32).astype(jnp.bfloat16)
        acts = aq_ref[...] * member
        for first in range(0, rows, sub):
            span = pl.ds(first, sub)
            outer = jnp.dot(grad_ref[span, :n_query], acts, preferred_element_type=jnp.float32)
            p_ref[span, :] = (outer * inv_ref[span, :]).astype(jnp.bfloat16)

    def score(s, p_ref):
        total = jnp.zeros((8, n_train), jnp.float32)
        for first in range(0, rows, sub):
            span = pl.ds(first, sub)
            mapped = jnp.dot(p_ref[span, :], au_ref[...], preferred_element_type=jnp.float32)
            weighted = mapped * wide_ref[span, :]
            total = total + jnp.sum(weighted.reshape(sub // 8, 8, n_train), axis=0)
        out_ref[pl.ds(s, 1), :] = jnp.sum(total, axis=0, keepdims=True)

    precondition(0, even_ref)

    def pair(k, carry):
        precondition(2 * k + 1, odd_ref)
        score(2 * k, even_ref)
        precondition(2 * k + 2, even_ref)
        score(2 * k + 1, odd_ref)
        return carry

    lax.fori_loop(0, n_seq // 2, pair, 0)


def score_chunk(damping, seq, grads_t, acts_q, acts_ut, eig):
    rows, cols = eig.shape
    n_query, n_train = acts_q.shape[0], acts_ut.shape[1]
    sub = min(rows, 512)
    flops = 2 * S * rows * cols * (n_query + n_train)
    return pl.pallas_call(
        functools.partial(score_kernel, S, n_query, sub),
        out_shape=jax.ShapeDtypeStruct((S, n_train), jnp.float32),
        in_specs=[pl.BlockSpec(memory_space=pltpu.SMEM)]
        + [pl.BlockSpec(memory_space=pltpu.VMEM)] * 5,
        out_specs=pl.BlockSpec(memory_space=pltpu.VMEM),
        scratch_shapes=[
            pltpu.VMEM((rows, cols), jnp.float32),
            pltpu.VMEM((rows, n_train), jnp.float32),
            pltpu.VMEM((rows, cols), jnp.bfloat16),
            pltpu.VMEM((rows, cols), jnp.bfloat16),
        ],
        compiler_params=pltpu.CompilerParams(vmem_limit_bytes=48 * 1024 * 1024),
        cost_estimate=pl.CostEstimate(
            flops=flops, bytes_accessed=rows * cols * 4, transcendentals=0
        ),
    )(damping, seq, grads_t, acts_q, acts_ut, eig)


def local(
    query_grads,
    query_acts,
    train_grads,
    train_acts,
    grad_basis,
    act_basis,
    eigen_corr,
    damping,
    query_seq,
    train_doc,
):
    f32, bf16 = jnp.float32, jnp.bfloat16
    gather = functools.partial(lax.all_gather, axis=0, tiled=True)
    acts_all = jnp.concatenate([gather(query_acts, "col"), gather(train_acts, "col")], axis=0)
    grads_all = jnp.concatenate([gather(query_grads, "row"), gather(train_grads, "row")], axis=0)
    n_col = lax.axis_size("col")
    n_query = query_seq.shape[0]
    row_block, col_block = eigen_corr.shape

    act_part = jnp.dot(acts_all, act_basis, preferred_element_type=f32)
    act_own = lax.psum_scatter(act_part, "row", scatter_dimension=0, tiled=True).astype(bf16)
    acts_rot = gather(act_own, "row")
    acts_q, acts_ut = acts_rot[:n_query], acts_rot[n_query:].T

    damp = damping.reshape(1, 1)
    seq = query_seq.reshape(n_query, 1)
    step = row_block // CHUNKS
    partial_scores = 0.0
    for chunk in range(CHUNKS):
        basis = grad_basis[:, chunk * step : (chunk + 1) * step]
        part = lax.dot_general(
            basis, grads_all, (((0,), (1,)), ((), ())), preferred_element_type=f32
        )
        own = lax.psum_scatter(part, "col", scatter_dimension=0, tiled=True).astype(bf16)
        grads_t = gather(own, "col")
        eig = eigen_corr[chunk * step : (chunk + 1) * step]
        partial_scores = partial_scores + score_chunk(damp, seq, grads_t, acts_q, acts_ut, eig)
    partial_scores = partial_scores / D

    doc_table = (train_doc[:, None] == jnp.arange(DOCS, dtype=jnp.int32)[None, :]).astype(f32)
    counts = jnp.sum(doc_table, axis=0)
    total = lax.psum(partial_scores, ("row", "col"))
    owned = total.shape[1] // n_col
    scores = lax.dynamic_slice_in_dim(total, lax.axis_index("col") * owned, owned, 1)
    doc_sum = jnp.dot(total, doc_table, precision=lax.Precision.HIGHEST)
    return (scores, doc_sum / counts[None, :])


def solution(mesh):
    in_specs = (
        P("row", "col"),
        P("col", "row"),
        P("row", "col"),
        P("col", "row"),
        P("col", "row"),
        P("row", "col"),
        P("row", "col"),
        P(),
        P(),
        P(),
    )
    out_specs = (P(None, "col"), P())
    return jax.shard_map(local, mesh=mesh, in_specs=in_specs, out_specs=out_specs, check_vma=False)
```

```python
import functools

import jax
import jax.numpy as jnp
from jax import lax
from jax.experimental import pallas as pl
from jax.experimental.pallas import tpu as pltpu
from jax.sharding import PartitionSpec as P

D = 8192
S = 32
DOCS = 16
CHUNKS = 4


def score_kernel(n_seq, n_query, sub, damp_ref, seq_ref, grad_ref, aq_ref, au_ref, eig_ref, out_ref,
                 inv_ref, wide_ref, even_ref, odd_ref):
    rows, cols = eig_ref.shape
    n_train = au_ref.shape[1]
    @pl.when(pl.program_id(0) == 0)
    def _():
        out_ref[...] = jnp.zeros_like(out_ref)

    inv_ref[...] = 1.0 / (eig_ref[...] + damp_ref[0, 0])
    wide_ref[...] = grad_ref[:, n_query:].astype(jnp.float32)

    def precondition(s, p_ref):
        member = (seq_ref[...] == s).astype(jnp.float32).astype(jnp.bfloat16)
        acts = aq_ref[...] * member
        for first in range(0, rows, sub):
            span = pl.ds(first, sub)
            outer = jnp.dot(grad_ref[span, :n_query], acts, preferred_element_type=jnp.float32)
            p_ref[span, :] = (outer * inv_ref[span, :]).astype(jnp.bfloat16)

    def score(s, p_ref):
        total = jnp.zeros((8, n_train), jnp.float32)
        for first in range(0, rows, sub):
            span = pl.ds(first, sub)
            mapped = jnp.dot(p_ref[span, :], au_ref[...], preferred_element_type=jnp.float32)
            weighted = mapped * wide_ref[span, :]
            total = total + jnp.sum(weighted.reshape(sub // 8, 8, n_train), axis=0)
        out_ref[pl.ds(s, 1), :] += jnp.sum(total, axis=0, keepdims=True)

    precondition(0, even_ref)

    def pair(k, carry):
        precondition(2 * k + 1, odd_ref)
        score(2 * k, even_ref)
        precondition(2 * k + 2, even_ref)
        score(2 * k + 1, odd_ref)
        return carry

    lax.fori_loop(0, n_seq // 2, pair, 0)


def block_scores(damping, seq, grads_t, acts_q, acts_ut, eig):
    rows, cols = eig.shape
    n_query, n_train = acts_q.shape[0], acts_ut.shape[1]
    step = rows // CHUNKS
    flops = 2 * S * rows * cols * (n_query + n_train)
    whole = lambda x: pl.BlockSpec(x.shape, lambda i: (0, 0))
    part = lambda x: pl.BlockSpec((step, x.shape[1]), lambda i: (i, 0))
    return pl.pallas_call(
        functools.partial(score_kernel, S, n_query, min(step, 512)),
        grid=(CHUNKS,),
        out_shape=jax.ShapeDtypeStruct((S, n_train), jnp.float32),
        in_specs=[
            pl.BlockSpec(memory_space=pltpu.SMEM),
            whole(seq),
            part(grads_t),
            whole(acts_q),
            whole(acts_ut),
            part(eig),
        ],
        out_specs=pl.BlockSpec((S, n_train), lambda i: (0, 0)),
        scratch_shapes=[
            pltpu.VMEM((step, cols), jnp.float32),
            pltpu.VMEM((step, n_train), jnp.float32),
            pltpu.VMEM((step, cols), jnp.bfloat16),
            pltpu.VMEM((step, cols), jnp.bfloat16),
        ],
        compiler_params=pltpu.CompilerParams(vmem_limit_bytes=48 * 1024 * 1024),
        cost_estimate=pl.CostEstimate(
            flops=flops, bytes_accessed=rows * cols * 4, transcendentals=0
        ),
    )(damping, seq, grads_t, acts_q, acts_ut, eig)


MESH = pl.DeviceIdType.MESH


def ring_place(axis, n):
    me = lax.axis_index(axis)
    odd = lax.rem(me, 2)
    place = (1 - odd) * (me // 2) + odd * ((2 * n - 1 - me) // 2)

    def device(position):
        p = lax.rem(position + 2 * n, n)
        back = p // (n // 2)
        return (1 - back) * (2 * p) + back * (2 * n - 1 - 2 * p)

    return me, place, device


def greet(peers):
    barrier = pltpu.get_barrier_semaphore()
    for peer in peers:
        pl.semaphore_signal(barrier, inc=1, device_id=peer, device_id_type=MESH)
    pl.semaphore_wait(barrier, len(peers))


def ring_peers(axes):
    peers = []
    for axis, n in axes:
        me, place, device = ring_place(axis, n)
        peers += [{axis: device(place + 1)}, {axis: device(place - 1)}]
    return peers


def gather_steps(axes, outs, send_sems, recv_sems):
    rings = [ring_place(axis, n) for axis, n in axes]
    sends = []
    for t in range(max(n for _, n in axes) - 1):
        current = []
        for k, (axis, n) in enumerate(axes):
            if t >= n - 1:
                continue
            me, place, device = rings[k]
            half = outs[k].shape[1] // 2
            for way, sign in enumerate((1, -1)):
                piece = outs[k].at[device(place - sign * t), pl.ds(way * half, half)]
                copy = pltpu.make_async_remote_copy(
                    src_ref=piece,
                    dst_ref=piece,
                    send_sem=send_sems[k].at[way, t],
                    recv_sem=recv_sems[k].at[way, t],
                    device_id={axis: device(place + sign)},
                    device_id_type=MESH,
                )
                copy.start()
                current.append(copy)
        for copy in current:
            copy.wait_recv()
        sends += current
    for copy in sends:
        copy.wait_send()


def gather_kernel(axes, *refs):
    k = len(axes)
    ins, outs, sems = refs[:k], refs[k : 2 * k], refs[2 * k :]
    for (axis, n), own, out in zip(axes, ins, outs):
        out[lax.axis_index(axis)] = own[...]
    greet(ring_peers(axes))
    gather_steps(axes, outs, sems[:k], sems[k:])


def sum_kernel(axes, *refs):
    k = len(axes)
    parts, outs, slots = refs[:k], refs[k : 2 * k], refs[2 * k : 3 * k]
    sems = refs[3 * k :]
    greet(ring_peers(axes))
    rings = [ring_place(axis, n) for axis, n in axes]
    sends = []
    for t in range(max(n for _, n in axes) - 1):
        current = []
        for j, (axis, n) in enumerate(axes):
            if t >= n - 1:
                continue
            me, place, device = rings[j]
            half = parts[j].shape[1] // 2
            for way, sign in enumerate((1, -1)):
                rows = pl.ds(way * half, half)
                piece = device(place - sign * (1 + t))
                if t == 0:
                    source = parts[j].at[piece, rows]
                else:
                    source = slots[j].at[way, t - 1]
                    slots[j][way, t - 1] = slots[j][way, t - 1] + parts[j][piece, rows]
                copy = pltpu.make_async_remote_copy(
                    src_ref=source,
                    dst_ref=slots[j].at[way, t],
                    send_sem=sems[j].at[way, t],
                    recv_sem=sems[k + j].at[way, t],
                    device_id={axis: device(place + sign)},
                    device_id_type=MESH,
                )
                copy.start()
                current.append(copy)
        for copy in current:
            copy.wait_recv()
        sends += current
    for copy in sends:
        copy.wait_send()
    for j, (axis, n) in enumerate(axes):
        me = rings[j][0]
        half = parts[j].shape[1] // 2
        for way in range(2):
            rows = pl.ds(way * half, half)
            outs[j][me, rows] = (slots[j][way, n - 2] + parts[j][me, rows]).astype(outs[j].dtype)
    gather_steps(axes, outs, sems[2 * k : 3 * k], sems[3 * k :])


def dma_sems(axes):
    return [pltpu.SemaphoreType.DMA((2, n - 1)) for _, n in axes]


def vmem_specs(k):
    return [pl.BlockSpec(memory_space=pltpu.VMEM)] * k


def ring_gather(axes, arrays):
    return pl.pallas_call(
        functools.partial(gather_kernel, axes),
        out_shape=[jax.ShapeDtypeStruct((n,) + x.shape, x.dtype) for (_, n), x in zip(axes, arrays)],
        in_specs=vmem_specs(len(axes)),
        out_specs=vmem_specs(len(axes)),
        scratch_shapes=dma_sems(axes) * 2,
        compiler_params=pltpu.CompilerParams(
            collective_id=0, has_side_effects=True, vmem_limit_bytes=40 * 1024 * 1024
        ),
    )(*arrays)


def ring_sum(axes, arrays):
    slots = [pltpu.VMEM((2, n - 1, x.shape[1] // 2, x.shape[2]), x.dtype) for (_, n), x in zip(axes, arrays)]
    return pl.pallas_call(
        functools.partial(sum_kernel, axes),
        out_shape=[jax.ShapeDtypeStruct(x.shape, jnp.bfloat16) for x in arrays],
        in_specs=vmem_specs(len(axes)),
        out_specs=vmem_specs(len(axes)),
        scratch_shapes=slots + dma_sems(axes) * 4,
        compiler_params=pltpu.CompilerParams(
            collective_id=1, has_side_effects=True, vmem_limit_bytes=40 * 1024 * 1024
        ),
    )(*arrays)


def total_kernel(axes, x_ref, out_ref, *refs):
    k = len(axes)
    slots, sems = refs[:k], refs[k:]
    peers = []
    for axis, n in axes:
        me = lax.axis_index(axis)
        peers.append([{axis: lax.rem(me + d, n)} for d in range(1, n)])
    greet(sum(peers, []))
    value = x_ref[...]
    for j, (axis, n) in enumerate(axes):
        me = lax.axis_index(axis)
        slots[j][me] = value
        copies = []
        for d in range(1, n):
            copy = pltpu.make_async_remote_copy(
                src_ref=slots[j].at[me],
                dst_ref=slots[j].at[me],
                send_sem=sems[j].at[d - 1],
                recv_sem=sems[k + j].at[d - 1],
                device_id=peers[j][d - 1],
                device_id_type=MESH,
            )
            copy.start()
            copies.append(copy)
        for copy in copies:
            copy.wait()
        value = slots[j][0]
        for d in range(1, n):
            value = value + slots[j][d]
    out_ref[...] = value


def total_sum(axes, x):
    sems = [pltpu.SemaphoreType.DMA((n - 1,)) for _, n in axes]
    return pl.pallas_call(
        functools.partial(total_kernel, axes),
        out_shape=jax.ShapeDtypeStruct(x.shape, x.dtype),
        in_specs=vmem_specs(1),
        out_specs=pl.BlockSpec(memory_space=pltpu.VMEM),
        scratch_shapes=[pltpu.VMEM((n,) + x.shape, x.dtype) for _, n in axes] + sems * 2,
        compiler_params=pltpu.CompilerParams(collective_id=2, has_side_effects=True),
    )(x)


def local(
    query_grads,
    query_acts,
    train_grads,
    train_acts,
    grad_basis,
    act_basis,
    eigen_corr,
    damping,
    query_seq,
    train_doc,
):
    f32, bf16 = jnp.float32, jnp.bfloat16
    n_row, n_col = lax.axis_size("row"), lax.axis_size("col")
    axes = (("col", n_col), ("row", n_row))
    n_query, n_train = query_seq.shape[0], train_doc.shape[0]
    row_block, col_block = eigen_corr.shape
    own_acts = jnp.concatenate([query_acts, train_acts], axis=0)
    own_grads = jnp.concatenate([query_grads, train_grads], axis=0)
    act_query, grad_query = query_acts.shape[0], query_grads.shape[0]
    pieces = (own_acts.shape[0], own_grads.shape[0], row_block // n_col, (n_query + n_train) // n_row)
    rings = n_row % 2 == 0 and n_col % 2 == 0 and all(size % 32 == 0 for size in pieces)

    def in_order(gathered, first):
        q, t = gathered[:, :first], gathered[:, first:]
        return jnp.concatenate([q.reshape(n_query, -1), t.reshape(n_train, -1)], axis=0)

    if rings:
        acts_all, grads_all = ring_gather(axes, (own_acts, own_grads))
    else:
        acts_all = lax.all_gather(own_acts, "col")
        grads_all = lax.all_gather(own_grads, "row")
    acts_all, grads_all = in_order(acts_all, act_query), in_order(grads_all, grad_query)
    act_part = jnp.dot(acts_all, act_basis, preferred_element_type=f32)
    grad_part = lax.dot_general(
        grad_basis, grads_all, (((0,), (1,)), ((), ())), preferred_element_type=f32
    )
    if rings:
        grads_t, acts_rot = ring_sum(
            axes,
            (
                grad_part.reshape(n_col, row_block // n_col, n_query + n_train),
                act_part.reshape(n_row, (n_query + n_train) // n_row, col_block),
            ),
        )
        grads_t = grads_t.reshape(row_block, n_query + n_train)
        acts_rot = acts_rot.reshape(n_query + n_train, col_block)
    else:
        grads_t = lax.psum(grad_part, "col").astype(bf16)
        acts_rot = lax.psum(act_part, "row").astype(bf16)
    acts_q, acts_ut = acts_rot[:n_query], acts_rot[n_query:].T

    damp = damping.reshape(1, 1)
    seq = query_seq.reshape(n_query, 1)
    partial_scores = block_scores(damp, seq, grads_t, acts_q, acts_ut, eigen_corr) / D

    doc_table = (train_doc[:, None] == jnp.arange(DOCS, dtype=jnp.int32)[None, :]).astype(f32)
    counts = jnp.sum(doc_table, axis=0)
    if rings:
        total = total_sum((("row", n_row), ("col", n_col)), partial_scores)
    else:
        total = lax.psum(partial_scores, ("row", "col"))
    owned = total.shape[1] // n_col
    scores = lax.dynamic_slice_in_dim(total, lax.axis_index("col") * owned, owned, 1)
    doc_sum = jnp.dot(total, doc_table, precision=lax.Precision.HIGHEST)
    return (scores, doc_sum / counts[None, :])


def solution(mesh):
    in_specs = (
        P("row", "col"),
        P("col", "row"),
        P("row", "col"),
        P("col", "row"),
        P("col", "row"),
        P("row", "col"),
        P("row", "col"),
        P(),
        P(),
        P(),
    )
    out_specs = (P(None, "col"), P())
    return jax.shard_map(local, mesh=mesh, in_specs=in_specs, out_specs=out_specs, check_vma=False)
```

```python
import functools

import jax
import jax.numpy as jnp
from jax import lax
from jax.experimental import pallas as pl
from jax.experimental.pallas import tpu as pltpu
from jax.sharding import PartitionSpec as P

D = 8192
S = 32
DOCS = 16
CHUNKS = 4


def score_kernel(n_seq, n_query, sub, damp_ref, seq_ref, grad_ref, aq_ref, au_ref, eig_ref, out_ref,
                 inv_ref, wide_ref, even_ref, odd_ref):
    rows, cols = eig_ref.shape
    n_train = au_ref.shape[1]
    @pl.when(pl.program_id(0) == 0)
    def _():
        out_ref[...] = jnp.zeros_like(out_ref)

    inv_ref[...] = 1.0 / (eig_ref[...] + damp_ref[0, 0])
    wide_ref[...] = grad_ref[:, n_query:].astype(jnp.float32)

    def precondition(s, p_ref):
        member = (seq_ref[...] == s).astype(jnp.float32).astype(jnp.bfloat16)
        acts = aq_ref[...] * member
        for first in range(0, rows, sub):
            span = pl.ds(first, sub)
            outer = jnp.dot(grad_ref[span, :n_query], acts, preferred_element_type=jnp.float32)
            p_ref[span, :] = (outer * inv_ref[span, :]).astype(jnp.bfloat16)

    def score(s, p_ref):
        total = jnp.zeros((8, n_train), jnp.float32)
        for first in range(0, rows, sub):
            span = pl.ds(first, sub)
            mapped = jnp.dot(p_ref[span, :], au_ref[...], preferred_element_type=jnp.float32)
            weighted = mapped * wide_ref[span, :]
            total = total + jnp.sum(weighted.reshape(sub // 8, 8, n_train), axis=0)
        out_ref[pl.ds(s, 1), :] += jnp.sum(total, axis=0, keepdims=True)

    precondition(0, even_ref)

    def pair(k, carry):
        precondition(2 * k + 1, odd_ref)
        score(2 * k, even_ref)
        precondition(2 * k + 2, even_ref)
        score(2 * k + 1, odd_ref)
        return carry

    lax.fori_loop(0, n_seq // 2, pair, 0)


def block_scores(damping, seq, grads_t, acts_q, acts_ut, eig):
    rows, cols = eig.shape
    n_query, n_train = acts_q.shape[0], acts_ut.shape[1]
    step = rows // CHUNKS
    flops = 2 * S * rows * cols * (n_query + n_train)
    whole = lambda x: pl.BlockSpec(x.shape, lambda i: (0, 0))
    part = lambda x: pl.BlockSpec((step, x.shape[1]), lambda i: (i, 0))
    return pl.pallas_call(
        functools.partial(score_kernel, S, n_query, min(step, 512)),
        grid=(CHUNKS,),
        out_shape=jax.ShapeDtypeStruct((S, n_train), jnp.float32),
        in_specs=[
            pl.BlockSpec(memory_space=pltpu.SMEM),
            whole(seq),
            part(grads_t),
            whole(acts_q),
            whole(acts_ut),
            part(eig),
        ],
        out_specs=pl.BlockSpec((S, n_train), lambda i: (0, 0)),
        scratch_shapes=[
            pltpu.VMEM((step, cols), jnp.float32),
            pltpu.VMEM((step, n_train), jnp.float32),
            pltpu.VMEM((step, cols), jnp.bfloat16),
            pltpu.VMEM((step, cols), jnp.bfloat16),
        ],
        compiler_params=pltpu.CompilerParams(vmem_limit_bytes=48 * 1024 * 1024),
        cost_estimate=pl.CostEstimate(
            flops=flops, bytes_accessed=rows * cols * 4, transcendentals=0
        ),
    )(damping, seq, grads_t, acts_q, acts_ut, eig)


MESH = pl.DeviceIdType.MESH


def ring_place(axis, n):
    me = lax.axis_index(axis)
    odd = lax.rem(me, 2)
    place = (1 - odd) * (me // 2) + odd * ((2 * n - 1 - me) // 2)

    def device(position):
        p = lax.rem(position + 2 * n, n)
        back = p // (n // 2)
        return (1 - back) * (2 * p) + back * (2 * n - 1 - 2 * p)

    return me, place, device


def greet(peers):
    barrier = pltpu.get_barrier_semaphore()
    for peer in peers:
        pl.semaphore_signal(barrier, inc=1, device_id=peer, device_id_type=MESH)
    pl.semaphore_wait(barrier, len(peers))


def ring_peers(axes):
    peers = []
    for axis, n in axes:
        me, place, device = ring_place(axis, n)
        peers += [{axis: device(place + 1)}, {axis: device(place - 1)}]
    return peers


def gather_steps(axes, outs, send_sems, recv_sems):
    rings = [ring_place(axis, n) for axis, n in axes]
    sends = []
    for t in range(max(n for _, n in axes) - 1):
        current = []
        for k, (axis, n) in enumerate(axes):
            if t >= n - 1:
                continue
            me, place, device = rings[k]
            half = outs[k].shape[1] // 2
            for way, sign in enumerate((1, -1)):
                piece = outs[k].at[device(place - sign * t), pl.ds(way * half, half)]
                copy = pltpu.make_async_remote_copy(
                    src_ref=piece,
                    dst_ref=piece,
                    send_sem=send_sems[k].at[way, t],
                    recv_sem=recv_sems[k].at[way, t],
                    device_id={axis: device(place + sign)},
                    device_id_type=MESH,
                )
                copy.start()
                current.append(copy)
        for copy in current:
            copy.wait_recv()
        sends += current
    for copy in sends:
        copy.wait_send()


def gather_kernel(axes, *refs):
    k = len(axes)
    ins, outs, sems = refs[:k], refs[k : 2 * k], refs[2 * k :]
    for (axis, n), own, out in zip(axes, ins, outs):
        out[lax.axis_index(axis)] = own[...]
    greet(ring_peers(axes))
    gather_steps(axes, outs, sems[:k], sems[k:])


def sum_kernel(axes, *refs):
    k = len(axes)
    parts, outs, slots = refs[:k], refs[k : 2 * k], refs[2 * k : 3 * k]
    sems = refs[3 * k :]
    greet(ring_peers(axes))
    rings = [ring_place(axis, n) for axis, n in axes]
    sends = []
    for t in range(max(n for _, n in axes) - 1):
        current = []
        for j, (axis, n) in enumerate(axes):
            if t >= n - 1:
                continue
            me, place, device = rings[j]
            half = parts[j].shape[1] // 2
            for way, sign in enumerate((1, -1)):
                rows = pl.ds(way * half, half)
                piece = device(place - sign * (1 + t))
                running = parts[j][piece, rows]
                if t > 0:
                    running = running + slots[j][way, t - 1].astype(jnp.float32)
                here = (t - 1) % n
                slots[j][way, here] = running.astype(slots[j].dtype)
                source = slots[j].at[way, here]
                copy = pltpu.make_async_remote_copy(
                    src_ref=source,
                    dst_ref=slots[j].at[way, t],
                    send_sem=sems[j].at[way, t],
                    recv_sem=sems[k + j].at[way, t],
                    device_id={axis: device(place + sign)},
                    device_id_type=MESH,
                )
                copy.start()
                current.append(copy)
        for copy in current:
            copy.wait_recv()
        sends += current
    for copy in sends:
        copy.wait_send()
    for j, (axis, n) in enumerate(axes):
        me = rings[j][0]
        half = parts[j].shape[1] // 2
        for way in range(2):
            rows = pl.ds(way * half, half)
            last = slots[j][way, n - 2].astype(jnp.float32)
            outs[j][me, rows] = (last + parts[j][me, rows]).astype(outs[j].dtype)
    gather_steps(axes, outs, sems[2 * k : 3 * k], sems[3 * k :])


def dma_sems(axes):
    return [pltpu.SemaphoreType.DMA((2, n - 1)) for _, n in axes]


def vmem_specs(k):
    return [pl.BlockSpec(memory_space=pltpu.VMEM)] * k


def ring_gather(axes, arrays):
    return pl.pallas_call(
        functools.partial(gather_kernel, axes),
        out_shape=[jax.ShapeDtypeStruct((n,) + x.shape, x.dtype) for (_, n), x in zip(axes, arrays)],
        in_specs=vmem_specs(len(axes)),
        out_specs=vmem_specs(len(axes)),
        scratch_shapes=dma_sems(axes) * 2,
        compiler_params=pltpu.CompilerParams(
            collective_id=0, has_side_effects=True, vmem_limit_bytes=40 * 1024 * 1024
        ),
    )(*arrays)


def ring_sum(axes, arrays, wires):
    slots = [
        pltpu.VMEM((2, n, x.shape[1] // 2, x.shape[2]), wire)
        for (_, n), x, wire in zip(axes, arrays, wires)
    ]
    return pl.pallas_call(
        functools.partial(sum_kernel, axes),
        out_shape=[jax.ShapeDtypeStruct(x.shape, jnp.bfloat16) for x in arrays],
        in_specs=vmem_specs(len(axes)),
        out_specs=vmem_specs(len(axes)),
        scratch_shapes=slots + dma_sems(axes) * 4,
        compiler_params=pltpu.CompilerParams(
            collective_id=1, has_side_effects=True, vmem_limit_bytes=40 * 1024 * 1024
        ),
    )(*arrays)


def total_kernel(axes, x_ref, out_ref, *refs):
    k = len(axes)
    slots, sems = refs[:k], refs[k:]
    peers = []
    for axis, n in axes:
        me = lax.axis_index(axis)
        peers.append([{axis: lax.rem(me + d, n)} for d in range(1, n)])
    greet(sum(peers, []))
    value = x_ref[...]
    for j, (axis, n) in enumerate(axes):
        me = lax.axis_index(axis)
        slots[j][me] = value
        copies = []
        for d in range(1, n):
            copy = pltpu.make_async_remote_copy(
                src_ref=slots[j].at[me],
                dst_ref=slots[j].at[me],
                send_sem=sems[j].at[d - 1],
                recv_sem=sems[k + j].at[d - 1],
                device_id=peers[j][d - 1],
                device_id_type=MESH,
            )
            copy.start()
            copies.append(copy)
        for copy in copies:
            copy.wait()
        value = slots[j][0]
        for d in range(1, n):
            value = value + slots[j][d]
    out_ref[...] = value


def total_sum(axes, x):
    sems = [pltpu.SemaphoreType.DMA((n - 1,)) for _, n in axes]
    return pl.pallas_call(
        functools.partial(total_kernel, axes),
        out_shape=jax.ShapeDtypeStruct(x.shape, x.dtype),
        in_specs=vmem_specs(1),
        out_specs=pl.BlockSpec(memory_space=pltpu.VMEM),
        scratch_shapes=[pltpu.VMEM((n,) + x.shape, x.dtype) for _, n in axes] + sems * 2,
        compiler_params=pltpu.CompilerParams(collective_id=2, has_side_effects=True),
    )(x)


def local(
    query_grads,
    query_acts,
    train_grads,
    train_acts,
    grad_basis,
    act_basis,
    eigen_corr,
    damping,
    query_seq,
    train_doc,
):
    f32, bf16 = jnp.float32, jnp.bfloat16
    n_row, n_col = lax.axis_size("row"), lax.axis_size("col")
    axes = (("col", n_col), ("row", n_row))
    n_query, n_train = query_seq.shape[0], train_doc.shape[0]
    row_block, col_block = eigen_corr.shape
    own_acts = jnp.concatenate([query_acts, train_acts], axis=0)
    own_grads = jnp.concatenate([query_grads, train_grads], axis=0)
    act_query, grad_query = query_acts.shape[0], query_grads.shape[0]
    pieces = (own_acts.shape[0], own_grads.shape[0], row_block // n_col, (n_query + n_train) // n_row)
    rings = n_row % 2 == 0 and n_col % 2 == 0 and all(size % 32 == 0 for size in pieces)

    def in_order(gathered, first):
        q, t = gathered[:, :first], gathered[:, first:]
        return jnp.concatenate([q.reshape(n_query, -1), t.reshape(n_train, -1)], axis=0)

    if rings:
        acts_all, grads_all = ring_gather(axes, (own_acts, own_grads))
    else:
        acts_all = lax.all_gather(own_acts, "col")
        grads_all = lax.all_gather(own_grads, "row")
    acts_all, grads_all = in_order(acts_all, act_query), in_order(grads_all, grad_query)
    act_part = jnp.dot(acts_all, act_basis, preferred_element_type=f32)
    grad_part = lax.dot_general(
        grad_basis, grads_all, (((0,), (1,)), ((), ())), preferred_element_type=f32
    )
    if rings:
        grads_t, acts_rot = ring_sum(
            axes,
            (
                grad_part.reshape(n_col, row_block // n_col, n_query + n_train),
                act_part.reshape(n_row, (n_query + n_train) // n_row, col_block),
            ),
            (bf16, f32),
        )
        grads_t = grads_t.reshape(row_block, n_query + n_train)
        acts_rot = acts_rot.reshape(n_query + n_train, col_block)
    else:
        grads_t = lax.psum(grad_part, "col").astype(bf16)
        acts_rot = lax.psum(act_part, "row").astype(bf16)
    acts_q, acts_ut = acts_rot[:n_query], acts_rot[n_query:].T

    damp = damping.reshape(1, 1)
    seq = query_seq.reshape(n_query, 1)
    partial_scores = block_scores(damp, seq, grads_t, acts_q, acts_ut, eigen_corr) / D

    doc_table = (train_doc[:, None] == jnp.arange(DOCS, dtype=jnp.int32)[None, :]).astype(f32)
    counts = jnp.sum(doc_table, axis=0)
    if rings:
        total = total_sum((("row", n_row), ("col", n_col)), partial_scores)
    else:
        total = lax.psum(partial_scores, ("row", "col"))
    owned = total.shape[1] // n_col
    scores = lax.dynamic_slice_in_dim(total, lax.axis_index("col") * owned, owned, 1)
    doc_sum = jnp.dot(total, doc_table, precision=lax.Precision.HIGHEST)
    return (scores, doc_sum / counts[None, :])


def solution(mesh):
    in_specs = (
        P("row", "col"),
        P("col", "row"),
        P("row", "col"),
        P("col", "row"),
        P("col", "row"),
        P("row", "col"),
        P("row", "col"),
        P(),
        P(),
        P(),
    )
    out_specs = (P(None, "col"), P())
    return jax.shard_map(local, mesh=mesh, in_specs=in_specs, out_specs=out_specs, check_vma=False)
```
